32 devices in a mesh: occ: 4 (over z), vir: 8 (over y, x, core).
Axes of the slice: x: 2, y: 2, z: 4, core: 2. Of those that a mesh axis runs over, the one named last changes fastest.
Arguments:
- amplitudes: bfloat16 [512, 6144], P('vir', 'occ'), may hold values from -6 to 6
- tiles: bfloat16 [4, 8, 48, 9216], P('occ', 'vir'), may hold values from -0.1875 to 0.1875
- tile_map: int32 [4, 8, 48], P('occ', 'vir'), may hold values from 0 to 128, as said below
Outputs:
- residual: bfloat16 [512, 6144], P('occ', 'vir')
The draws below stay inside these ranges and needn't reach their ends.
Inputs may be any that keep to these rules, and one draw needn't show every extreme that they name: `tile_map`: in each device's list of 48 slots the live entries name distinct tile pairs and come first; the value 16 * 8 marks an empty slot; some device has all 48 slots live.
All inputs are finite; a program needn't handle non-finite values.
Results may differ from the reference program's by a relative error of at most 0.022.
Values may be sent and summed in bfloat16 or wider, within the bound.
No kernel may reach another device: no remote copies, remote signals or barrier semaphores. Data moves between devices by JAX's collectives and lax.ppermute only.
A program may use at most 64 MiB of HBM per device.

```python
import jax
import jax.numpy as jnp
from jax import lax

TILE = 96
CON_TILES = 16
RES_TILES = 8
SLOTS = 48
ROWS = 512
CD_PAIRS = 6144
AB_PAIRS = 6144
N_OCC = 4
N_VIR = 8


def draw_tile_map(key, part):
    devices = N_OCC * N_VIR
    pairs = CON_TILES * RES_TILES
    keys = jax.random.split(jax.random.fold_in(key, 11), devices)
    orders = jax.vmap(lambda single: jax.random.permutation(single, pairs)[:SLOTS])(keys)
    live = jax.random.randint(jax.random.fold_in(key, 12), (devices,), SLOTS // 5, SLOTS + 1)
    fullest = jax.random.randint(jax.random.fold_in(key, 13), (), 0, devices)
    live = jnp.where(jnp.arange(devices) == fullest, SLOTS, live)
    positions = jnp.arange(SLOTS)
    result = jnp.where(positions[None, :] < live[:, None], orders, pairs)
    return result.reshape(N_OCC, N_VIR, SLOTS).astype(jnp.int32)


def level_of(stream_key, shape, pieces, low, high):
    def one(axis_at, shards_of):
        steps = jax.random.uniform(jax.random.fold_in(jax.random.fold_in(stream_key, 6), axis_at), (shards_of,), jnp.float32, low / len(pieces), high / len(pieces))
        return jnp.repeat(jnp.exp(steps), shape[axis_at] // shards_of).reshape((-1,) + (1,) * (len(shape) - axis_at - 1))

    level = one(*pieces[0])
    for cut in pieces[1:]:
        level = level * one(*cut)
    return level


def noise(stream_key, extent, scale, reach, cuts=(), kind=jnp.bfloat16):
    loudness = level_of(stream_key, extent, cuts, -0.22, 0.18) if cuts else 1.0
    array = jax.random.normal(stream_key, extent, jnp.float32) * scale * loudness
    return jnp.minimum(jnp.maximum(array, -reach), reach).astype(kind)


def setup_inputs(seed: int = 0) -> dict:
    splits = jax.random.split(jax.random.key(seed), 4)
    amplitudes = noise(splits[0], (ROWS, CD_PAIRS), 1.0, 6.0, ((0, 8), (1, 4)))
    tiles = noise(splits[1], (N_OCC, N_VIR, SLOTS, TILE * TILE), (TILE * N_OCC * SLOTS // (2 * RES_TILES)) ** -0.5, 0.1875, ((0, 4), (1, 8)))
    tile_map = draw_tile_map(jax.random.fold_in(splits[3], 71), 0)
    return dict(amplitudes=amplitudes, tiles=tiles, tile_map=tile_map)


def reference(amplitudes, tiles, tile_map):
    pair_ids = jnp.arange(CON_TILES * RES_TILES, dtype=jnp.int32)

    def add_block(running, inputs):
        amp_block, tile_block, map_block = inputs
        onehot = (map_block[:, :, None] == pair_ids[None, None, :]).astype(jnp.float32)
        placed = jnp.einsum("vsp,vsq->vpq", onehot, tile_block.astype(jnp.float32))
        placed = placed.astype(jnp.bfloat16).reshape(N_VIR, CON_TILES, RES_TILES, TILE, TILE)
        placed = placed.transpose(1, 3, 0, 2, 4).reshape(CON_TILES * TILE, N_VIR * RES_TILES * TILE)
        partial_value = jnp.dot(amp_block, placed, preferred_element_type=jnp.float32)
        rounded = lax.optimization_barrier(partial_value.astype(jnp.bfloat16))
        return running + rounded.astype(jnp.float32), None

    amp_blocks = amplitudes.reshape(ROWS, N_OCC, CON_TILES * TILE).transpose(1, 0, 2)
    start_sum = jnp.zeros((ROWS, AB_PAIRS), jnp.float32)
    totals, unused = lax.scan(add_block, start_sum, (amp_blocks, tiles, tile_map))
    return totals.astype(jnp.bfloat16)
```

```python
import functools

import jax
import jax.numpy as jnp
from jax import lax
from jax.experimental import pallas as pl
from jax.experimental.pallas import tpu as pltpu
from jax.sharding import PartitionSpec as P

TILE = 96
CON_TILES = 16
RES_TILES = 8
LANES = 128
PERIOD = 384
LINES = TILE * TILE // PERIOD
CON = CON_TILES * TILE
RES = RES_TILES * TILE
CUTS = (0, 64)


def densify_kernel(map_ref, tiles_ref, dense_ref, flat_ref, square_ref, slot_ref):
    slots = tiles_ref.shape[0]
    for line in range(3 * LINES):
        flat_ref[line % 3, pl.ds(line // 3, slots, stride=LINES), :] = tiles_ref[
            :, line * LANES : (line + 1) * LANES
        ].astype(jnp.float32)

    def clear(pair, carry):
        slot_ref[pair] = slots
        return carry

    lax.fori_loop(0, CON_TILES * RES_TILES + 1, clear, 0, unroll=8)
    square_ref[slots] = jnp.zeros((TILE, LANES), jnp.float32)
    lane = lax.broadcasted_iota(jnp.int32, (LINES, LANES), 1)

    def shape_slot(slot, carry):
        pair = map_ref[slot]
        slot_ref[pair] = slot
        turn = lax.rem(lax.rem(pair, RES_TILES) * TILE, LANES)
        rows = pl.ds(pl.multiple_of(slot * LINES, 8), LINES)
        x0, x1, x2 = flat_ref[0, rows, :], flat_ref[1, rows, :], flat_ref[2, rows, :]
        parts = (
            x0,
            jnp.where(lane >= 96, x0, x1),
            jnp.where(lane >= 64, x1, x2),
            x2,
        )
        for i, part in enumerate(parts):
            square_ref[slot, pl.ds(i, LINES, stride=4), :] = pltpu.roll(
                part, lax.rem(turn + 32 * i, LANES), 1
            )
        return carry

    lax.fori_loop(0, slots, shape_slot, 0, unroll=4)
    lane = lax.broadcasted_iota(jnp.int32, (TILE, LANES), 1)

    def place(con, carry):
        rows = pl.ds(pl.multiple_of(con * TILE, TILE), TILE)
        for half in range(2):
            p = [square_ref[slot_ref[con * RES_TILES + 4 * half + i]] for i in range(4)]
            out = (
                jnp.where(lane < 96, p[0], p[1]),
                jnp.where(lane < 64, p[1], p[2]),
                jnp.where(lane < 32, p[2], p[3]),
            )
            for i in range(3):
                at = (3 * half + i) * LANES
                dense_ref[rows, at : at + LANES] = out[i].astype(jnp.bfloat16)
        return carry

    lax.fori_loop(0, CON_TILES, place, 0, unroll=2)


def densify(tiles, tile_map):
    slots = tiles.shape[2]
    return pl.pallas_call(
        densify_kernel,
        out_shape=jax.ShapeDtypeStruct((CON, RES), jnp.bfloat16),
        in_specs=[
            pl.BlockSpec(memory_space=pltpu.SMEM),
            pl.BlockSpec(memory_space=pltpu.VMEM),
        ],
        out_specs=pl.BlockSpec(memory_space=pltpu.VMEM),
        scratch_shapes=[
            pltpu.VMEM((3, slots * LINES, LANES), jnp.float32),
            pltpu.VMEM((slots + 1, TILE, LANES), jnp.float32),
            pltpu.SMEM((CON_TILES * RES_TILES + 8,), jnp.int32),
        ],
        compiler_params=pltpu.CompilerParams(vmem_limit_bytes=24 * 2**20),
        cost_estimate=pl.CostEstimate(flops=6 * 10**8, bytes_accessed=8 * 10**6, transcendentals=0),
        name="densify",
    )(tile_map.reshape(slots), tiles.reshape(slots, TILE * TILE))


def ladder_kernel(chips, *refs):
    blocks, dense_ref = refs[: 2 * chips], refs[2 * chips]
    outs, rows_ref = refs[2 * chips + 1 : -1], refs[-1]
    vir = lax.axis_index("vir")
    chip, core, occ = vir // 2, lax.rem(vir, 2), lax.axis_index("occ")
    for k in range(chips):
        at = jnp.bitwise_xor(jnp.bitwise_xor(chip, k), occ)
        rows_ref[at, core] = blocks[2 * k][...]
        rows_ref[at, 1 - core] = blocks[2 * k + 1][...]
    height = rows_ref.shape[2]
    for k in range(chips):
        lhs = rows_ref[k].reshape(2 * height, CON)
        out = jnp.dot(lhs, dense_ref[...], preferred_element_type=jnp.float32)
        outs[k][...] = out.astype(jnp.bfloat16)


def ladder(blocks, dense):
    chips = len(blocks) // 2
    height = blocks[0].shape[0]
    vmem = pl.BlockSpec(memory_space=pltpu.VMEM)
    return pl.pallas_call(
        functools.partial(ladder_kernel, chips),
        out_shape=[jax.ShapeDtypeStruct((2 * height, RES), jnp.bfloat16)] * chips,
        in_specs=[vmem] * (2 * chips + 1),
        out_specs=[vmem] * chips,
        scratch_shapes=[pltpu.VMEM((chips, 2, height, CON), jnp.bfloat16)],
        compiler_params=pltpu.CompilerParams(vmem_limit_bytes=40 * 2**20),
        cost_estimate=pl.CostEstimate(
            flops=4 * chips * height * CON * RES, bytes_accessed=6 * 10**6, transcendentals=0
        ),
        name="ladder",
    )(*blocks, dense)


def swap(value, axis, size, mask):
    return lax.ppermute(value, axis, [(i, i ^ mask) for i in range(size)])


def per_device(n_occ, n_vir, amplitudes, tiles, tile_map):
    dense = densify(tiles, tile_map)
    parts = []
    for low, high in zip(CUTS, CUTS[1:]):
        mine = amplitudes[low:high]
        held = [mine] + [swap(mine, "vir", n_vir, 2 * k) for k in range(1, n_vir // 2)]
        blocks = []
        for block in held:
            blocks += [block, swap(block, "vir", n_vir, 1)]
        outs = ladder(blocks, dense)
        terms = [outs[0]] + [swap(outs[k], "occ", n_occ, k) for k in range(1, n_occ)]
        total = sum(term.astype(jnp.float32) for term in terms).astype(jnp.bfloat16)
        parts.append(total.reshape(2, high - low, RES))
    return jnp.concatenate(parts, axis=1).reshape(-1, RES)


def solution(mesh):
    in_specs = (P("vir", "occ"), P("occ", "vir", None, None), P("occ", "vir", None))
    out_specs = P("occ", "vir")
    return jax.shard_map(
        functools.partial(per_device, mesh.shape["occ"], mesh.shape["vir"]),
        mesh=mesh,
        in_specs=in_specs,
        out_specs=out_specs,
        check_vma=False,
    )
```

```python
import functools

import jax
import jax.numpy as jnp
from jax import lax
from jax.experimental import pallas as pl
from jax.experimental.pallas import tpu as pltpu
from jax.sharding import PartitionSpec as P

TILE = 96
CON_TILES = 16
RES_TILES = 8
LANES = 128
PERIOD = 384
LINES = TILE * TILE // PERIOD
CON = CON_TILES * TILE
RES = RES_TILES * TILE


def densify_kernel(map_ref, tiles_ref, dense_ref, flat_ref, square_ref, slot_ref):
    slots = tiles_ref.shape[0]
    for line in range(3 * LINES):
        flat_ref[line % 3, pl.ds(line // 3, slots, stride=LINES), :] = tiles_ref[
            :, line * LANES : (line + 1) * LANES
        ].astype(jnp.float32)

    def clear(pair, carry):
        slot_ref[pair] = slots
        return carry

    lax.fori_loop(0, CON_TILES * RES_TILES + 1, clear, 0, unroll=8)
    square_ref[slots] = jnp.zeros((TILE, LANES), jnp.float32)
    lane = lax.broadcasted_iota(jnp.int32, (LINES, LANES), 1)

    def shape_slot(slot, carry):
        pair = map_ref[slot]
        slot_ref[pair] = slot
        turn = lax.rem(lax.rem(pair, RES_TILES) * TILE, LANES)
        rows = pl.ds(pl.multiple_of(slot * LINES, 8), LINES)
        x0, x1, x2 = flat_ref[0, rows, :], flat_ref[1, rows, :], flat_ref[2, rows, :]
        parts = (
            x0,
            jnp.where(lane >= 96, x0, x1),
            jnp.where(lane >= 64, x1, x2),
            x2,
        )
        for i, part in enumerate(parts):
            square_ref[slot, pl.ds(i, LINES, stride=4), :] = pltpu.roll(
                part, lax.rem(turn + 32 * i, LANES), 1
            )
        return carry

    lax.fori_loop(0, slots, shape_slot, 0, unroll=4)
    lane = lax.broadcasted_iota(jnp.int32, (TILE, LANES), 1)

    def place(con, carry):
        rows = pl.ds(pl.multiple_of(con * TILE, TILE), TILE)
        for half in range(2):
            p = [square_ref[slot_ref[con * RES_TILES + 4 * half + i]] for i in range(4)]
            out = (
                jnp.where(lane < 96, p[0], p[1]),
                jnp.where(lane < 64, p[1], p[2]),
                jnp.where(lane < 32, p[2], p[3]),
            )
            for i in range(3):
                at = (3 * half + i) * LANES
                dense_ref[rows, at : at + LANES] = out[i].astype(jnp.bfloat16)
        return carry

    lax.fori_loop(0, CON_TILES, place, 0, unroll=2)


def densify(tiles, tile_map):
    slots = tiles.shape[2]
    return pl.pallas_call(
        densify_kernel,
        out_shape=jax.ShapeDtypeStruct((CON, RES), jnp.bfloat16),
        in_specs=[
            pl.BlockSpec(memory_space=pltpu.SMEM),
            pl.BlockSpec(memory_space=pltpu.VMEM),
        ],
        out_specs=pl.BlockSpec(memory_space=pltpu.VMEM),
        scratch_shapes=[
            pltpu.VMEM((3, slots * LINES, LANES), jnp.float32),
            pltpu.VMEM((slots + 1, TILE, LANES), jnp.float32),
            pltpu.SMEM((CON_TILES * RES_TILES + 8,), jnp.int32),
        ],
        compiler_params=pltpu.CompilerParams(vmem_limit_bytes=24 * 2**20),
        cost_estimate=pl.CostEstimate(flops=6 * 10**8, bytes_accessed=8 * 10**6, transcendentals=0),
        name="densify",
    )(tile_map.reshape(slots), tiles.reshape(slots, TILE * TILE))


def ladder_kernel(chips, *refs):
    blocks, dense_ref = refs[:chips], refs[chips]
    own_ref, near_ref, keep_ref, send_ref, rows_ref = refs[chips + 1 :]
    chip, occ = lax.axis_index("vir") // 2, lax.axis_index("occ")
    for m in range(chips):
        rows_ref[jnp.bitwise_xor(jnp.bitwise_xor(chip, m), occ)] = blocks[m][...]
    height = rows_ref.shape[1]
    for k in range(0, chips, 4):
        lhs = rows_ref[k : k + 4].reshape(4 * height, CON)
        out = jnp.dot(lhs, dense_ref[...], preferred_element_type=jnp.float32)
        out = out.astype(jnp.bfloat16).reshape(4, height, RES)
        for i in range(4):
            if k + i == 0:
                own_ref[...] = out[i]
            elif k + i == 1:
                near_ref[...] = out[i]
            else:
                (keep_ref, send_ref)[i % 2][(k + i) // 2 - 1] = out[i]


def ladder(blocks, dense):
    chips = len(blocks)
    height = blocks[0].shape[0]
    vmem = pl.BlockSpec(memory_space=pltpu.VMEM)
    one = jax.ShapeDtypeStruct((height, RES), jnp.bfloat16)
    far = jax.ShapeDtypeStruct((chips // 2 - 1, height, RES), jnp.bfloat16)
    return pl.pallas_call(
        functools.partial(ladder_kernel, chips),
        out_shape=[one, one, far, far],
        in_specs=[vmem] * (chips + 1),
        out_specs=[vmem] * 4,
        scratch_shapes=[pltpu.VMEM((chips, height, CON), jnp.bfloat16)],
        compiler_params=pltpu.CompilerParams(vmem_limit_bytes=32 * 2**20),
        cost_estimate=pl.CostEstimate(
            flops=2 * chips * height * CON * RES, bytes_accessed=6 * 10**6, transcendentals=0
        ),
        name="ladder",
    )(*blocks, dense)


def swap(value, axis, size, mask):
    return lax.ppermute(value, axis, [(i, i ^ mask) for i in range(size)])


def add(*terms):
    return sum(term.astype(jnp.float32) for term in terms)


def per_device(n_occ, n_vir, amplitudes, tiles, tile_map):
    dense = densify(tiles, tile_map)
    chips = n_vir // 2
    held = [amplitudes] + [None] * (chips - 1)
    for m in list(range(2, chips)) + [1]:
        held[m] = swap(amplitudes, "vir", n_vir, 2 * m)
    *held, dense = lax.optimization_barrier((*held, dense))
    other = [swap(block, "vir", n_vir, 1) for block in held]
    own, near, far = [], [], []
    for blocks in (held, other):
        own_part, near_part, keep, send = ladder(blocks, dense)
        got = swap(send, "occ", n_occ, 1)
        pair = add(keep, got).astype(jnp.bfloat16)
        own.append(own_part)
        near.append(near_part)
        far.append([swap(pair[i], "occ", n_occ, 2 * i + 2) for i in range(n_occ // 2 - 1)])
    near = swap(jnp.concatenate(near, axis=0), "occ", n_occ, 1)
    height = own[0].shape[0]
    near = [near[:height], near[height:]]
    first, second = [add(own[i], near[i], *far[i]).astype(jnp.bfloat16) for i in range(2)]
    core = lax.rem(lax.axis_index("vir"), 2)
    return jnp.where(
        core == 0,
        jnp.concatenate([first, second], axis=0),
        jnp.concatenate([second, first], axis=0),
    )


def solution(mesh):
    in_specs = (P("vir", "occ"), P("occ", "vir", None, None), P("occ", "vir", None))
    out_specs = P("occ", "vir")
    return jax.shard_map(
        functools.partial(per_device, mesh.shape["occ"], mesh.shape["vir"]),
        mesh=mesh,
        in_specs=in_specs,
        out_specs=out_specs,
        check_vma=False,
    )
```

```python
import functools

import jax
import jax.numpy as jnp
from jax import lax
from jax.experimental import pallas as pl
from jax.experimental.pallas import tpu as pltpu
from jax.sharding import PartitionSpec as P

TILE = 96
CON_TILES = 16
RES_TILES = 8
LANES = 128
PERIOD = 384
LINES = TILE * TILE // PERIOD
CON = CON_TILES * TILE
RES = RES_TILES * TILE


def densify_kernel(map_ref, tiles_ref, dense_ref, flat_ref, square_ref, slot_ref):
    slots = tiles_ref.shape[0]
    for line in range(3 * LINES):
        flat_ref[line % 3, pl.ds(line // 3, slots, stride=LINES), :] = tiles_ref[
            :, line * LANES : (line + 1) * LANES
        ].astype(jnp.float32)

    def clear(pair, carry):
        slot_ref[pair] = slots
        return carry

    lax.fori_loop(0, CON_TILES * RES_TILES + 1, clear, 0, unroll=8)
    square_ref[slots] = jnp.zeros((TILE, LANES), jnp.float32)
    lane = lax.broadcasted_iota(jnp.int32, (LINES, LANES), 1)

    def shape_slot(slot, carry):
        pair = map_ref[slot]
        slot_ref[pair] = slot
        turn = lax.rem(lax.rem(pair, RES_TILES) * TILE, LANES)
        rows = pl.ds(pl.multiple_of(slot * LINES, 8), LINES)
        x0, x1, x2 = flat_ref[0, rows, :], flat_ref[1, rows, :], flat_ref[2, rows, :]
        parts = (
            x0,
            jnp.where(lane >= 96, x0, x1),
            jnp.where(lane >= 64, x1, x2),
            x2,
        )
        for i, part in enumerate(parts):
            square_ref[slot, pl.ds(i, LINES, stride=4), :] = pltpu.roll(
                part, lax.rem(turn + 32 * i, LANES), 1
            )
        return carry

    lax.fori_loop(0, slots, shape_slot, 0, unroll=4)
    lane = lax.broadcasted_iota(jnp.int32, (TILE, LANES), 1)

    def place(con, carry):
        rows = pl.ds(pl.multiple_of(con * TILE, TILE), TILE)
        for half in range(2):
            p = [square_ref[slot_ref[con * RES_TILES + 4 * half + i]] for i in range(4)]
            out = (
                jnp.where(lane < 96, p[0], p[1]),
                jnp.where(lane < 64, p[1], p[2]),
                jnp.where(lane < 32, p[2], p[3]),
            )
            for i in range(3):
                at = (3 * half + i) * LANES
                dense_ref[rows, at : at + LANES] = out[i].astype(jnp.bfloat16)
        return carry

    lax.fori_loop(0, CON_TILES, place, 0, unroll=2)


def densify(tiles, tile_map):
    slots = tiles.shape[2]
    return pl.pallas_call(
        densify_kernel,
        out_shape=jax.ShapeDtypeStruct((CON, RES), jnp.bfloat16),
        in_specs=[
            pl.BlockSpec(memory_space=pltpu.SMEM),
            pl.BlockSpec(memory_space=pltpu.VMEM),
        ],
        out_specs=pl.BlockSpec(memory_space=pltpu.VMEM),
        scratch_shapes=[
            pltpu.VMEM((3, slots * LINES, LANES), jnp.float32),
            pltpu.VMEM((slots + 1, TILE, LANES), jnp.float32),
            pltpu.SMEM((CON_TILES * RES_TILES + 8,), jnp.int32),
        ],
        compiler_params=pltpu.CompilerParams(vmem_limit_bytes=24 * 2**20),
        cost_estimate=pl.CostEstimate(flops=6 * 10**8, bytes_accessed=8 * 10**6, transcendentals=0),
        name="densify",
    )(tile_map.reshape(slots), tiles.reshape(slots, TILE * TILE))


def ladder_kernel(chips, *refs):
    blocks, dense_ref = refs[:chips], refs[chips]
    own_ref, near_ref, keep_ref, send_ref, rows_ref = refs[chips + 1 :]
    chip, occ = lax.axis_index("vir") // 2, lax.axis_index("occ")
    for m in range(chips):
        rows_ref[jnp.bitwise_xor(jnp.bitwise_xor(chip, m), occ)] = blocks[m][...]
    height = rows_ref.shape[1]
    for k in range(0, chips, 4):
        lhs = rows_ref[k : k + 4].reshape(4 * height, CON)
        out = jnp.dot(lhs, dense_ref[...], preferred_element_type=jnp.float32)
        out = out.astype(jnp.bfloat16).reshape(4, height, RES)
        for i in range(4):
            if k + i == 0:
                own_ref[...] = out[i]
            elif k + i == 1:
                near_ref[...] = out[i]
            else:
                (keep_ref, send_ref)[i % 2][(k + i) // 2 - 1] = out[i]


def ladder(blocks, dense):
    chips = len(blocks)
    height = blocks[0].shape[0]
    vmem = pl.BlockSpec(memory_space=pltpu.VMEM)
    one = jax.ShapeDtypeStruct((height, RES), jnp.bfloat16)
    far = jax.ShapeDtypeStruct((chips // 2 - 1, height, RES), jnp.bfloat16)
    return pl.pallas_call(
        functools.partial(ladder_kernel, chips),
        out_shape=[one, one, far, far],
        in_specs=[vmem] * (chips + 1),
        out_specs=[vmem] * 4,
        scratch_shapes=[pltpu.VMEM((chips, height, CON), jnp.bfloat16)],
        compiler_params=pltpu.CompilerParams(vmem_limit_bytes=32 * 2**20),
        cost_estimate=pl.CostEstimate(
            flops=2 * chips * height * CON * RES, bytes_accessed=6 * 10**6, transcendentals=0
        ),
        name="ladder",
    )(*blocks, dense)


def swap(value, axis, size, mask):
    return lax.ppermute(value, axis, [(i, i ^ mask) for i in range(size)])


def add(*terms):
    return sum(term.astype(jnp.float32) for term in terms)


def per_device(n_occ, n_vir, amplitudes, tiles, tile_map):
    dense = densify(tiles, tile_map)
    chips = n_vir // 2
    held = [amplitudes] + [None] * (chips - 1)
    for m in list(range(2, chips)) + [1]:
        held[m] = swap(amplitudes, "vir", n_vir, 2 * m)
    *held, dense = lax.optimization_barrier((*held, dense))
    other = [swap(block, "vir", n_vir, 1) for block in held]
    parts = [ladder(blocks, dense) for blocks in (held, other)]
    got = [swap(send, "occ", n_occ, 1) for _, _, _, send in parts]
    got[0], parts[1] = lax.optimization_barrier((got[0], parts[1]))
    own, near, far = [], [], []
    for (own_part, near_part, keep, _), received in zip(parts, got):
        pair = add(keep, received).astype(jnp.bfloat16)
        own.append(own_part)
        near.append(near_part)
        far.append([swap(pair[i], "occ", n_occ, 2 * i + 2) for i in range(n_occ // 2 - 1)])
    near = swap(jnp.concatenate(near, axis=0), "occ", n_occ, 1)
    height = own[0].shape[0]
    near = [near[:height], near[height:]]
    first, second = [add(own[i], near[i], *far[i]).astype(jnp.bfloat16) for i in range(2)]
    core = lax.rem(lax.axis_index("vir"), 2)
    return jnp.where(
        core == 0,
        jnp.concatenate([first, second], axis=0),
        jnp.concatenate([second, first], axis=0),
    )


def solution(mesh):
    in_specs = (P("vir", "occ"), P("occ", "vir", None, None), P("occ", "vir", None))
    out_specs = P("occ", "vir")
    return jax.shard_map(
        functools.partial(per_device, mesh.shape["occ"], mesh.shape["vir"]),
        mesh=mesh,
        in_specs=in_specs,
        out_specs=out_specs,
        check_vma=False,
    )
```

```python
import functools

import jax
import jax.numpy as jnp
from jax import lax
from jax.experimental import pallas as pl
from jax.experimental.pallas import tpu as pltpu
from jax.sharding import PartitionSpec as P

TILE = 96
CON_TILES = 16
RES_TILES = 8
LANES = 128
PERIOD = 384
LINES = TILE * TILE // PERIOD
PIECES = 6
CON = CON_TILES * TILE
RES = RES_TILES * TILE


def densify_kernel(
    map_hbm, tiles_hbm, dense_ref, tiles_ref, flat_ref, square_ref, map_ref, slot_ref, sems
):
    slots = tiles_ref.shape[0]
    width = tiles_ref.shape[1] // PIECES
    map_copy = pltpu.make_async_copy(map_hbm, map_ref, sems.at[PIECES])
    copies = [
        pltpu.make_async_copy(
            tiles_hbm.at[:, pl.ds(i * width, width)],
            tiles_ref.at[:, pl.ds(i * width, width)],
            sems.at[i],
        )
        for i in range(PIECES)
    ]
    map_copy.start()
    for copy in copies:
        copy.start()

    def clear(pair, carry):
        slot_ref[pair] = slots
        return carry

    lax.fori_loop(0, CON_TILES * RES_TILES + 1, clear, 0, unroll=16)
    empty = pl.ds(slots * TILE, TILE)
    square_ref[empty, :] = jnp.zeros((TILE, LANES), jnp.float32)
    map_copy.wait()

    def invert(slot, carry):
        slot_ref[map_ref[slot]] = slot
        return carry

    lax.fori_loop(0, slots, invert, 0, unroll=8)
    for i, copy in enumerate(copies):
        copy.wait()
        for line in range(i * 3 * LINES // PIECES, (i + 1) * 3 * LINES // PIECES):
            flat_ref[line % 3, pl.ds(line // 3, slots, stride=LINES), :] = tiles_ref[
                :, line * LANES : (line + 1) * LANES
            ].astype(jnp.float32)
    x0, x1, x2 = [flat_ref[i, : slots * LINES] for i in range(3)]
    lane = lax.broadcasted_iota(jnp.int32, x0.shape, 1)
    parts = (
        x0,
        pltpu.roll(jnp.where(lane >= 96, x0, x1), 32, 1),
        pltpu.roll(jnp.where(lane >= 64, x1, x2), 64, 1),
        pltpu.roll(x2, 96, 1),
    )
    for i, part in enumerate(parts):
        square_ref[pl.ds(i, slots * LINES, stride=4), :] = part
    lane = lax.broadcasted_iota(jnp.int32, (TILE, LANES), 1)

    def place(con, carry):
        rows = pl.ds(pl.multiple_of(con * TILE, TILE), TILE)
        for half in range(2):
            p = []
            for i in range(4):
                at = slot_ref[con * RES_TILES + 4 * half + i] * TILE
                tile = square_ref[pl.ds(pl.multiple_of(at, TILE), TILE), :]
                p.append(pltpu.roll(tile, LANES - 32 * i, 1) if i else tile)
            out = (
                jnp.where(lane < 96, p[0], p[1]),
                jnp.where(lane < 64, p[1], p[2]),
                jnp.where(lane < 32, p[2], p[3]),
            )
            for i in range(3):
                at = (3 * half + i) * LANES
                dense_ref[rows, at : at + LANES] = out[i].astype(jnp.bfloat16)
        return carry

    lax.fori_loop(0, CON_TILES, place, 0, unroll=True)


def densify(tiles, tile_map):
    slots = tiles.shape[2]
    return pl.pallas_call(
        densify_kernel,
        out_shape=jax.ShapeDtypeStruct((CON, RES), jnp.bfloat16),
        in_specs=[pl.BlockSpec(memory_space=pltpu.HBM)] * 2,
        out_specs=pl.BlockSpec(memory_space=pltpu.VMEM),
        scratch_shapes=[
            pltpu.VMEM((slots, TILE * TILE), jnp.bfloat16),
            pltpu.VMEM((3, (slots + 1) * LINES, LANES), jnp.float32),
            pltpu.VMEM(((slots + 1) * TILE, LANES), jnp.float32),
            pltpu.SMEM((slots,), jnp.int32),
            pltpu.SMEM((CON_TILES * RES_TILES + 8,), jnp.int32),
            pltpu.SemaphoreType.DMA((PIECES + 1,)),
        ],
        compiler_params=pltpu.CompilerParams(vmem_limit_bytes=24 * 2**20),
        cost_estimate=pl.CostEstimate(flops=6 * 10**8, bytes_accessed=0, transcendentals=0),
        name="densify",
    )(
        pltpu.with_memory_space_constraint(tile_map.reshape(slots), pltpu.HBM),
        pltpu.with_memory_space_constraint(tiles.reshape(slots, TILE * TILE), pltpu.HBM),
    )


def ladder_kernel(chips, *refs):
    blocks, dense_ref = refs[:chips], refs[chips]
    outs, rows_ref = refs[chips + 1 : -1], refs[-1]
    chip, occ = lax.axis_index("vir") // 2, lax.axis_index("occ")
    for m in range(chips):
        rows_ref[jnp.bitwise_xor(jnp.bitwise_xor(chip, m), occ)] = blocks[m][...]
    height = rows_ref.shape[1]
    for k in range(0, chips, 4):
        lhs = rows_ref[k : k + 4].reshape(4 * height, CON)
        out = jnp.dot(lhs, dense_ref[...], preferred_element_type=jnp.float32)
        out = out.astype(jnp.bfloat16).reshape(4, height, RES)
        for i in range(4):
            outs[k + i][...] = out[i]


def ladder(blocks, dense):
    chips = len(blocks)
    height = blocks[0].shape[0]
    vmem = pl.BlockSpec(memory_space=pltpu.VMEM)
    return pl.pallas_call(
        functools.partial(ladder_kernel, chips),
        out_shape=[jax.ShapeDtypeStruct((height, RES), jnp.bfloat16)] * chips,
        in_specs=[vmem] * (chips + 1),
        out_specs=[vmem] * chips,
        scratch_shapes=[pltpu.VMEM((chips, height, CON), jnp.bfloat16)],
        compiler_params=pltpu.CompilerParams(vmem_limit_bytes=32 * 2**20),
        cost_estimate=pl.CostEstimate(flops=10**11, bytes_accessed=0, transcendentals=0),
        name="ladder",
    )(*blocks, dense)


def swap(value, axis, size, mask):
    return lax.ppermute(value, axis, [(i, i ^ mask) for i in range(size)])


def add(*terms):
    return sum(term.astype(jnp.float32) for term in terms)


def per_device(n_occ, n_vir, amplitudes, tiles, tile_map):
    chips = n_vir // 2
    height = amplitudes.shape[0]
    swap_occ = functools.partial(swap, axis="occ", size=n_occ)
    swap_vir = functools.partial(swap, axis="vir", size=n_vir)
    dense = densify(tiles, tile_map)
    held = [amplitudes] + [None] * (chips - 1)
    for m in range(chips - 1, 0, -1):
        held[m] = swap_vir(amplitudes, mask=2 * m)
    dense, *held[1:] = lax.optimization_barrier((dense, *held[1:]))
    sibling = swap_vir(amplitudes, mask=1)
    dense, sibling = lax.optimization_barrier((dense, sibling))
    first = ladder(held, dense)
    first, *held[1:] = lax.optimization_barrier((first, *held[1:]))
    rest = swap_vir(jnp.concatenate(held[1:], axis=0), mask=1)
    other = [sibling] + [rest[(m - 1) * height : m * height] for m in range(1, chips)]
    second = ladder(other, dense)
    got = [{k: swap_occ(part[k + 1], mask=1) for k in range(2, n_occ, 2)} for part in (first, second)]
    near = [first[1], second[1]]
    near[1], got[1] = lax.optimization_barrier((near[1], got[1]))
    near = swap_occ(jnp.concatenate(near, axis=0), mask=1)
    near = [near[:height], near[height:]]
    pairs = [
        {k: add(part[k], pair).astype(jnp.bfloat16) for k, pair in received.items()}
        for part, received in zip((first, second), got)
    ]
    sums = [[swap_occ(pair, mask=k) for k, pair in part.items()] for part in pairs]
    first, second = [
        add(part[0], near[i], *sums[i]).astype(jnp.bfloat16) for i, part in enumerate((first, second))
    ]
    core = lax.rem(lax.axis_index("vir"), 2)
    return jnp.where(
        core == 0,
        jnp.concatenate([first, second], axis=0),
        jnp.concatenate([second, first], axis=0),
    )


def solution(mesh):
    in_specs = (P("vir", "occ"), P("occ", "vir", None, None), P("occ", "vir", None))
    out_specs = P("occ", "vir")
    return jax.shard_map(
        functools.partial(per_device, mesh.shape["occ"], mesh.shape["vir"]),
        mesh=mesh,
        in_specs=in_specs,
        out_specs=out_specs,
        check_vma=False,
    )
```

```python
import functools

import jax
import jax.numpy as jnp
from jax import lax
from jax.experimental import pallas as pl
from jax.experimental.pallas import tpu as pltpu
from jax.sharding import PartitionSpec as P

TILE = 96
CON_TILES = 16
RES_TILES = 8
LANES = 128
PERIOD = 384
LINES = TILE * TILE // PERIOD
PIECES = 6
CON = CON_TILES * TILE
RES = RES_TILES * TILE


def densify_kernel(
    map_hbm, tiles_hbm, dense_ref, tiles_ref, flat_ref, square_ref, map_ref, slot_ref, sems
):
    slots = tiles_ref.shape[0]
    width = tiles_ref.shape[1] // PIECES
    map_copy = pltpu.make_async_copy(map_hbm, map_ref, sems.at[PIECES])
    copies = [
        pltpu.make_async_copy(
            tiles_hbm.at[:, pl.ds(i * width, width)],
            tiles_ref.at[:, pl.ds(i * width, width)],
            sems.at[i],
        )
        for i in range(PIECES)
    ]
    map_copy.start()
    for copy in copies:
        copy.start()

    def clear(pair, carry):
        slot_ref[pair] = slots
        return carry

    lax.fori_loop(0, CON_TILES * RES_TILES + 1, clear, 0, unroll=16)
    empty = pl.ds(slots * TILE, TILE)
    square_ref[empty, :] = jnp.zeros((TILE, LANES), jnp.float32)
    map_copy.wait()

    def invert(slot, carry):
        slot_ref[map_ref[slot]] = slot
        return carry

    lax.fori_loop(0, slots, invert, 0, unroll=8)
    for i, copy in enumerate(copies):
        copy.wait()
        for line in range(i * 3 * LINES // PIECES, (i + 1) * 3 * LINES // PIECES):
            flat_ref[line % 3, pl.ds(line // 3, slots, stride=LINES), :] = tiles_ref[
                :, line * LANES : (line + 1) * LANES
            ].astype(jnp.float32)
    x0, x1, x2 = [flat_ref[i, : slots * LINES] for i in range(3)]
    lane = lax.broadcasted_iota(jnp.int32, x0.shape, 1)
    parts = (
        x0,
        pltpu.roll(jnp.where(lane >= 96, x0, x1), 32, 1),
        pltpu.roll(jnp.where(lane >= 64, x1, x2), 64, 1),
        pltpu.roll(x2, 96, 1),
    )
    for i, part in enumerate(parts):
        square_ref[pl.ds(i, slots * LINES, stride=4), :] = part
    lane = lax.broadcasted_iota(jnp.int32, (TILE, LANES), 1)

    def place(con, carry):
        rows = pl.ds(pl.multiple_of(con * TILE, TILE), TILE)
        for half in range(2):
            p = []
            for i in range(4):
                at = slot_ref[con * RES_TILES + 4 * half + i] * TILE
                tile = square_ref[pl.ds(pl.multiple_of(at, TILE), TILE), :]
                p.append(pltpu.roll(tile, LANES - 32 * i, 1) if i else tile)
            out = (
                jnp.where(lane < 96, p[0], p[1]),
                jnp.where(lane < 64, p[1], p[2]),
                jnp.where(lane < 32, p[2], p[3]),
            )
            for i in range(3):
                at = (3 * half + i) * LANES
                dense_ref[rows, at : at + LANES] = out[i].astype(jnp.bfloat16)
        return carry

    lax.fori_loop(0, CON_TILES, place, 0, unroll=True)


def densify(tiles, tile_map):
    slots = tiles.shape[2]
    return pl.pallas_call(
        densify_kernel,
        out_shape=jax.ShapeDtypeStruct((CON, RES), jnp.bfloat16),
        in_specs=[pl.BlockSpec(memory_space=pltpu.HBM)] * 2,
        out_specs=pl.BlockSpec(memory_space=pltpu.VMEM),
        scratch_shapes=[
            pltpu.VMEM((slots, TILE * TILE), jnp.bfloat16),
            pltpu.VMEM((3, (slots + 1) * LINES, LANES), jnp.float32),
            pltpu.VMEM(((slots + 1) * TILE, LANES), jnp.float32),
            pltpu.SMEM((slots,), jnp.int32),
            pltpu.SMEM((CON_TILES * RES_TILES + 8,), jnp.int32),
            pltpu.SemaphoreType.DMA((PIECES + 1,)),
        ],
        compiler_params=pltpu.CompilerParams(vmem_limit_bytes=24 * 2**20),
        cost_estimate=pl.CostEstimate(flops=6 * 10**8, bytes_accessed=0, transcendentals=0),
        name="densify",
    )(
        pltpu.with_memory_space_constraint(tile_map.reshape(slots), pltpu.HBM),
        pltpu.with_memory_space_constraint(tiles.reshape(slots, TILE * TILE), pltpu.HBM),
    )


def ladder_kernel(chips, *refs):
    blocks, dense_ref = refs[:chips], refs[chips]
    outs, rows_ref = refs[chips + 1 : -1], refs[-1]
    chip, occ = lax.axis_index("vir") // 2, lax.axis_index("occ")
    for m in range(chips):
        rows_ref[jnp.bitwise_xor(jnp.bitwise_xor(chip, m), occ)] = blocks[m][...]
    height = rows_ref.shape[1]
    for k in range(0, chips, 4):
        lhs = rows_ref[k : k + 4].reshape(4 * height, CON)
        out = jnp.dot(lhs, dense_ref[...], preferred_element_type=jnp.float32)
        out = out.astype(jnp.bfloat16).reshape(4, height, RES)
        for i in range(4):
            outs[k + i][...] = out[i]


def ladder(blocks, dense):
    chips = len(blocks)
    height = blocks[0].shape[0]
    vmem = pl.BlockSpec(memory_space=pltpu.VMEM)
    return pl.pallas_call(
        functools.partial(ladder_kernel, chips),
        out_shape=[jax.ShapeDtypeStruct((height, RES), jnp.bfloat16)] * chips,
        in_specs=[vmem] * (chips + 1),
        out_specs=[vmem] * chips,
        scratch_shapes=[pltpu.VMEM((chips, height, CON), jnp.bfloat16)],
        compiler_params=pltpu.CompilerParams(vmem_limit_bytes=32 * 2**20),
        cost_estimate=pl.CostEstimate(flops=10**11, bytes_accessed=0, transcendentals=0),
        name="ladder",
    )(*blocks, dense)


def swap(value, axis, size, mask):
    return lax.ppermute(value, axis, [(i, i ^ mask) for i in range(size)])


def add(*terms):
    return sum(term.astype(jnp.float32) for term in terms)


def per_device(n_occ, n_vir, amplitudes, tiles, tile_map):
    chips = n_vir // 2
    height = amplitudes.shape[0]
    swap_occ = functools.partial(swap, axis="occ", size=n_occ)
    swap_vir = functools.partial(swap, axis="vir", size=n_vir)
    dense = densify(tiles, tile_map)
    held = [amplitudes] + [None] * (chips - 1)
    for m in range(chips - 1, 0, -1):
        held[m] = swap_vir(amplitudes, mask=2 * m)
    dense, *held[1:] = lax.optimization_barrier((dense, *held[1:]))
    sibling = swap_vir(amplitudes, mask=1)
    dense, sibling = lax.optimization_barrier((dense, sibling))
    first = ladder(held, dense)
    first, *held[1:] = lax.optimization_barrier((first, *held[1:]))
    rest = swap_vir(jnp.concatenate(held[1:], axis=0), mask=1)
    other = [sibling] + [rest[(m - 1) * height : m * height] for m in range(1, chips)]
    second = ladder(other, dense)
    got = [{k: swap_occ(part[k + 1], mask=1) for k in range(2, n_occ, 2)} for part in (first, second)]
    near = [first[1], second[1]]
    near[1], got[1] = lax.optimization_barrier((near[1], got[1]))
    near = swap_occ(jnp.concatenate(near, axis=0), mask=1)
    near = [near[:height], near[height:]]
    pairs = [
        {k: add(part[k], pair).astype(jnp.bfloat16) for k, pair in received.items()}
        for part, received in zip((first, second), got)
    ]
    sums = [[swap_occ(pair, mask=k) for k, pair in part.items()] for part in pairs]
    first, second = [
        add(part[0], near[i], *sums[i]).astype(jnp.bfloat16) for i, part in enumerate((first, second))
    ]
    core = lax.rem(lax.axis_index("vir"), 2)
    top, bottom = jnp.where(core == 0, first, second), jnp.where(core == 0, second, first)
    return jnp.concatenate([top, bottom], axis=0)


def solution(mesh):
    in_specs = (P("vir", "occ"), P("occ", "vir", None, None), P("occ", "vir", None))
    out_specs = P("occ", "vir")
    return jax.shard_map(
        functools.partial(per_device, mesh.shape["occ"], mesh.shape["vir"]),
        mesh=mesh,
        in_specs=in_specs,
        out_specs=out_specs,
        check_vma=False,
    )
```
